32 devices in a mesh: outer: 8 (over z, y), inner: 4 (over x, core).
Axes of the slice: x: 2, y: 2, z: 4, core: 2. Of those that a mesh axis runs over, the one named last changes fastest.
Arguments:
- queries: bfloat16 [8192, 1536], P(('outer', 'inner')), may hold values from -8 to 8
- key_rows: bfloat16 [8192, 1536], P(('outer', 'inner')), may hold values from -8 to 8
- value_rows: bfloat16 [8192, 1536], P(('outer', 'inner')), may hold values from -6 to 6
- upstream: bfloat16 [8192, 1536], P(('outer', 'inner')), may hold values from -6 to 6
- short_offsets: int32 [16], replicated, may hold values from 0 to 1
- global_offsets: int32 [16], replicated, may hold values from 0 to 15
Outputs:
- grad_queries: bfloat16 [8192, 1536], P(('outer', 'inner'))
- grad_keys: bfloat16 [8192, 1536], P(('outer', 'inner'))
- grad_values: bfloat16 [8192, 1536], P(('outer', 'inner'))
The draws below stay inside these ranges and needn't reach their ends.
All inputs are finite; a program needn't handle non-finite values.
Results may differ from the reference program's by a relative error of at most 0.006.
The reference program's roundings to bfloat16 on the way count: a program that leaves them out, or rounds other values in their place, can miss the bound.
Values may be sent and summed in bfloat16 or wider, within the bound.
A program may use at most 128 MiB of HBM per device.

```python
import jax
import jax.numpy as jnp
from jax import lax

H = 16
HD = 96
D = 1536
KEEP_B = 512
TOKENS = 8192
SEG = 1024
RATE_A = 2
RATE_B = 16
N_OUTER = 8


def drawn_rows(key, salt):
    base = jax.random.normal(jax.random.fold_in(key, salt), (TOKENS, D), jnp.float32)
    rows = jnp.clip(base, -6.0, 6.0)
    return rows.astype(jnp.bfloat16)


def draw_queries(key, part):
    return drawn_rows(key, 1)


def draw_key_rows(key, part):
    return drawn_rows(key, 2)


def with_ends(entries, own_key, smallest, top_value):
    longest = entries.shape.index(max(entries.shape))
    spots = []
    for shift in (0, 1):
        where = [jax.random.randint(jax.random.fold_in(own_key, axis), (), 0, length) for axis, length in enumerate(entries.shape)]
        where[longest] = (where[longest] + shift) % entries.shape[longest]
        spots.append(tuple(where))
    return entries.at[spots[0]].set(smallest).at[spots[1]].set(top_value)


def steps_of(key, extent, shards, low, largest):
    gain, own = 1.0, jax.random.fold_in(key, 6)
    for dim, shards_of in shards:
        draws = jnp.exp(jax.random.uniform(jax.random.fold_in(own, dim), (shards_of,), jnp.float32, low / len(shards), largest / len(shards)))
        gain = gain * jnp.repeat(draws, extent[dim] // shards_of).reshape([-1 if axis == dim else 1 for axis in range(len(extent))])
    return gain


def centred(rng, shape, scale, reach, pieces=(), kind=jnp.bfloat16):
    result = jax.random.normal(rng, shape, jnp.float32) * scale
    if len(pieces) > 0:
        result = steps_of(rng, shape, pieces, -0.22, 0.18) * result
    return jnp.clip(result, min=-reach, max=reach).astype(kind)


def setup_inputs(seed: int = 0) -> dict:
    splits = jax.random.split(jax.random.key(seed), 7)
    queries = draw_queries(jax.random.fold_in(splits[6], 71), 0)
    key_rows = draw_key_rows(jax.random.fold_in(splits[6], 71), 0)
    value_rows = centred(splits[2], (TOKENS, D), 1.0, 6.0, ((0, 32),))
    upstream = centred(splits[3], (TOKENS, D), 1.0, 6.0, ((0, 32),))
    short_offsets = with_ends(jax.random.randint(splits[4], (H,), 0, RATE_A), jax.random.fold_in(splits[4], 1), 0, RATE_A - 1).astype(jnp.int32)
    global_offsets = with_ends(jax.random.randint(splits[5], (H,), 0, RATE_B), jax.random.fold_in(splits[5], 1), 0, RATE_B - 1).astype(jnp.int32)
    return dict(queries=queries, key_rows=key_rows, value_rows=value_rows, upstream=upstream, short_offsets=short_offsets, global_offsets=global_offsets)


def pick_rows(block, offsets, stride):
    count = block.shape[0] // stride
    shaped = block.reshape(count, stride, H, HD)
    onehot = (jnp.arange(stride, dtype=jnp.int32)[:, None] == offsets[None, :]).astype(block.dtype)
    return jnp.sum(shaped * onehot[None, :, :, None], axis=1)


def put_rows(grads, offsets, stride):
    onehot = (jnp.arange(stride, dtype=jnp.int32)[:, None] == offsets[None, :]).astype(jnp.float32)
    spread = grads[:, None, :, :] * onehot[None, :, :, None]
    return spread.reshape(grads.shape[0] * stride, H * HD)


def attend_back(query_part, key_part, value_part, grad_part):
    softmax_scale = HD ** -0.5
    qf = query_part.astype(jnp.float32)
    kf = key_part.astype(jnp.float32)
    vf = value_part.astype(jnp.float32)
    gf = grad_part.astype(jnp.float32)
    scores = jnp.einsum('qhd,khd->hqk', qf, kf) * softmax_scale
    row_max = jnp.max(scores, axis=-1, keepdims=True)
    weights = jnp.exp(scores - row_max)
    probs = weights / jnp.sum(weights, axis=-1, keepdims=True)
    probs_low = probs.astype(jnp.bfloat16).astype(jnp.float32)
    output = jnp.einsum('hqk,khd->qhd', probs_low, vf)
    delta = jnp.sum(gf * output, axis=-1)
    dprobs = jnp.einsum('qhd,khd->hqk', gf, vf)
    dscores = (probs * (dprobs - jnp.transpose(delta)[:, :, None])).astype(jnp.bfloat16).astype(jnp.float32)
    grad_q = jnp.einsum('hqk,khd->qhd', dscores, kf) * softmax_scale
    grad_k = jnp.einsum('hqk,qhd->khd', dscores, qf) * softmax_scale
    grad_v = jnp.einsum('hqk,qhd->khd', probs_low, gf)
    return grad_q, grad_k, grad_v


def reference(queries, key_rows, value_rows, upstream, short_offsets, global_offsets):
    far = [pick_rows(member, global_offsets, RATE_B) for member in (queries, key_rows, value_rows, upstream)]
    far_grads = attend_back(far[0], far[1], far[2], far[3])
    per_seg = KEEP_B // N_OUTER
    far_split = [member.reshape(N_OUTER, per_seg, H, HD) for member in far_grads]
    blocks = [member.reshape(N_OUTER, SEG, D) for member in (queries, key_rows, value_rows, upstream)]

    def segment(pack):
        near = [pick_rows(pack[index], short_offsets, RATE_A) for index in range(4)]
        near_grads = attend_back(near[0], near[1], near[2], near[3])
        results = []
        for index in range(3):
            total = put_rows(near_grads[index], short_offsets, RATE_A) + put_rows(pack[4 + index], global_offsets, RATE_B)
            results.append(total.astype(jnp.bfloat16))
        return results[0], results[1], results[2]

    out_q, out_k, out_v = lax.map(segment, (blocks[0], blocks[1], blocks[2], blocks[3], far_split[0], far_split[1], far_split[2]))
    return out_q.reshape(TOKENS, D), out_k.reshape(TOKENS, D), out_v.reshape(TOKENS, D)
```

```python
import functools
import math

import jax
import jax.numpy as jnp
from jax import lax
from jax.experimental import pallas as pl
from jax.experimental.pallas import tpu as pltpu
from jax.sharding import PartitionSpec as P

H = 16
HD = 96
D = 1536
KEEP_A = 512
KEEP_B = 512
LANES = 128
MESH = pl.DeviceIdType.MESH


def pick_rows(block, offsets, stride):
    count = block.shape[0] // stride
    shaped = block.reshape(count, stride, H, HD)
    onehot = (jnp.arange(stride, dtype=jnp.int32)[:, None] == offsets[None, :]).astype(block.dtype)
    return jnp.sum(shaped * onehot[None, :, :, None], axis=1)


def put_rows(grads, offsets, stride):
    onehot = (jnp.arange(stride, dtype=jnp.int32)[:, None] == offsets[None, :]).astype(jnp.float32)
    spread = grads[:, None, :, :] * onehot[None, :, :, None]
    return spread.reshape(grads.shape[0] * stride, H * HD)


def attend_back(query_part, key_part, value_part, grad_part):
    softmax_scale = HD ** (-0.5)
    scores = (
        jnp.einsum("qhd,khd->hqk", query_part, key_part, preferred_element_type=jnp.float32)
        * softmax_scale
    )
    row_max = jnp.max(scores, axis=-1, keepdims=True)
    weights = jnp.exp(scores - row_max)
    probs = weights / jnp.sum(weights, axis=-1, keepdims=True)
    probs_low = probs.astype(jnp.bfloat16)
    output = jnp.einsum("hqk,khd->qhd", probs_low, value_part, preferred_element_type=jnp.float32)
    delta = jnp.sum(grad_part.astype(jnp.float32) * output, axis=-1)
    dprobs = jnp.einsum("qhd,khd->hqk", grad_part, value_part, preferred_element_type=jnp.float32)
    dscores = (probs * (dprobs - jnp.transpose(delta)[:, :, None])).astype(jnp.bfloat16)
    grad_q = (
        jnp.einsum("hqk,khd->qhd", dscores, key_part, preferred_element_type=jnp.float32)
        * softmax_scale
    )
    grad_k = (
        jnp.einsum("hqk,qhd->khd", dscores, query_part, preferred_element_type=jnp.float32)
        * softmax_scale
    )
    grad_v = jnp.einsum("hqk,qhd->khd", probs_low, grad_part, preferred_element_type=jnp.float32)
    return (grad_q, grad_k, grad_v)


def general(arrays, short_offsets, global_offsets, short_stride, far_stride, n_dev):
    far_count = arrays[0].shape[0] // far_stride
    near = [pick_rows(member, short_offsets, short_stride) for member in arrays]
    split = [lax.all_to_all(m, "inner", split_axis=1, concat_axis=0, tiled=True) for m in near]
    near_grads = attend_back(*split)
    near_final = [
        lax.all_to_all(m, "inner", split_axis=0, concat_axis=1, tiled=True) for m in near_grads
    ]
    far = [pick_rows(m, global_offsets, far_stride).reshape(far_count, D) for m in arrays]
    gathered = [
        lax.all_gather(m, ("outer", "inner"), axis=0, tiled=True).reshape(KEEP_B, 4, H // 4, HD)
        for m in far
    ]
    packed = tuple(jnp.moveaxis(m, 1, 0) for m in gathered)
    mapped = lax.map(lambda pack: attend_back(*pack), packed)
    whole = [jnp.moveaxis(m, 0, 1).reshape(KEEP_B, H, HD) for m in mapped]
    start = lax.axis_index(("outer", "inner")) * far_count
    results = []
    for index in range(3):
        mine = lax.dynamic_slice_in_dim(whole[index], start, far_count, 0)
        total = put_rows(near_final[index], short_offsets, short_stride) + put_rows(
            mine, global_offsets, far_stride
        )
        results.append(total.astype(jnp.bfloat16))
    return tuple(results)


def dot(a, b, dims):
    return lax.dot_general(a, b, (dims, ((), ())), preferred_element_type=jnp.float32)


def head_back(q, k, v, g, km, qm, gm):
    scale = HD ** (-0.5)
    s = dot(km, q, ((1,), (1,)))
    m = jnp.max(s, axis=0, keepdims=True)
    w = jnp.exp2((s - m) * (scale * math.log2(math.e)))
    p = w * (1.0 / jnp.sum(w, axis=0, keepdims=True))
    pb = p.astype(jnp.bfloat16)
    dp = dot(v, gm, ((1,), (1,)))
    delta = jnp.sum(pb.astype(jnp.float32) * dp, axis=0, keepdims=True)
    ds = (p * (dp - delta)).astype(jnp.bfloat16)
    dq = dot(ds, km, ((0,), (0,))) * scale
    dk = dot(ds, qm, ((1,), (0,))) * scale
    dv = dot(pb, gm, ((1,), (0,)))
    return dq.astype(jnp.bfloat16), dk.astype(jnp.bfloat16), dv.astype(jnp.bfloat16)


def picker(count, rows, stride):
    i = lax.broadcasted_iota(jnp.int32, (count, rows), 0)
    r = lax.broadcasted_iota(jnp.int32, (count, rows), 1)
    return (r // stride == i).astype(jnp.bfloat16)


def kernel(
    n_out, n_in, stride_a, stride_b,
    x0, x1, x2, x3, offs, o0, o1, o2,
    send_a, recv_a, ret_s, ret_r, send_b, recv_b, bret_s, bret_r,
    sa_sem, ra_sem, sr_sem, rr_sem, sb_sem, rb_sem, sbr_sem, rbr_sem,
):
    xs, outs = (x0, x1, x2, x3), (o0, o1, o2)
    n_dev = n_out * n_in
    spacing = n_dev // H
    mo, me = lax.axis_index("outer"), lax.axis_index("inner")
    mine = mo * n_in + me
    rows = x0.shape[0]
    na, nb = rows // stride_a, rows // stride_b
    width = D // n_in
    tiles = width // LANES
    heads = H // n_in
    far_head = mine // spacing
    is_far = mine % spacing == 0

    def place(index):
        return (index // n_in, index % n_in)

    barrier = pltpu.get_barrier_semaphore()

    def greet(step, carry):
        pl.semaphore_signal(
            barrier, inc=1, device_id=place((mine + step) % n_dev), device_id_type=MESH
        )
        return carry

    lax.fori_loop(1, n_dev, greet, 0)

    row_of = lax.broadcasted_iota(jnp.int32, (rows, LANES), 0)
    pick_a, pick_b = picker(na, rows, stride_a), picker(nb, rows, stride_b)

    off_b = offs[1:2, :]
    rows_b = lax.broadcasted_iota(jnp.int32, (rows, D), 0) % stride_b
    mask_b = (rows_b == off_b).astype(jnp.float32).astype(jnp.bfloat16)
    for a in range(4):
        far = dot(pick_b, xs[a][...] * mask_b, ((1,), (0,))).astype(jnp.bfloat16)
        for h in range(H):
            piece = far[:, h * HD:(h + 1) * HD]
            send_b[h, a] = jnp.concatenate(
                [piece, jnp.zeros((nb, LANES - HD), jnp.bfloat16)], axis=1
            )

    pl.semaphore_wait(barrier, n_dev - 1)

    def far_copy(h):
        return pltpu.make_async_remote_copy(
            src_ref=send_b.at[h], dst_ref=recv_b.at[mine], send_sem=sb_sem.at[h],
            recv_sem=rb_sem.at[mine], device_id=place(h * spacing), device_id_type=MESH,
        )

    def far_start(h, carry):
        @pl.when(h * spacing != mine)
        def _():
            far_copy(h).start()
        return carry

    lax.fori_loop(0, H, far_start, 0)

    def near_copy(t, step):
        peer = (me + step) % n_in
        return pltpu.make_async_remote_copy(
            src_ref=send_a.at[t, peer], dst_ref=recv_a.at[t, :, me],
            send_sem=sa_sem.at[t, step - 1], recv_sem=ra_sem.at[t, step - 1],
            device_id=(mo, peer), device_id_type=MESH,
        )

    row_a = row_of % stride_a
    for t in range(tiles):
        for p in range(n_in):
            c = p * width + t * LANES
            mask = (row_a == offs[0:1, c:c + LANES]).astype(jnp.float32).astype(jnp.bfloat16)
            for a in range(4):
                send_a[t, p, a] = dot(
                    pick_a, xs[a][:, c:c + LANES] * mask, ((1,), (0,))
                ).astype(jnp.bfloat16)
        for step in range(1, n_in):
            near_copy(t, step).start()
        for a in range(4):
            recv_a[t, a, me] = send_a[t, me, a]

    def back_copy(t, step):
        peer = (me + step) % n_in
        return pltpu.make_async_remote_copy(
            src_ref=ret_s.at[t, :, peer], dst_ref=ret_r.at[t, me],
            send_sem=sr_sem.at[t, step - 1], recv_sem=rr_sem.at[t, step - 1],
            device_id=(mo, peer), device_id_type=MESH,
        )

    def near_head(i, first):
        lo, hi = i * HD, (i + 1) * HD
        t0, t1 = lo // LANES, (hi - 1) // LANES
        wide = (t1 - t0 + 1) * LANES
        lane = lax.broadcasted_iota(jnp.int32, (1, wide), 1)
        mask = ((lane >= lo - t0 * LANES) & (lane < hi - t0 * LANES)).astype(jnp.float32)
        mask = mask.astype(jnp.bfloat16)

        def whole(a):
            parts = [recv_a[t, a].reshape(n_in * na, LANES) for t in range(t0, t1 + 1)]
            return jnp.concatenate(parts, axis=1) if len(parts) > 1 else parts[0]

        q, k, v, g = (whole(a) for a in range(4))
        grads = head_back(q, k, v, g, k * mask, q * mask, g * mask)
        for index, grad in enumerate(grads):
            for t in range(t0, t1 + 1):
                part = grad[:, (t - t0) * LANES:(t - t0 + 1) * LANES]
                part = part.reshape(n_in, na, LANES)
                if t in first:
                    part = part + ret_s[t, index]
                ret_s[t, index] = part
        first.update(range(t0, t1 + 1))

    def far_wait(j, carry):
        @pl.when(j != mine)
        def _():
            pltpu.make_async_remote_copy(
                src_ref=send_b.at[0], dst_ref=recv_b.at[j], send_sem=sb_sem.at[0],
                recv_sem=rb_sem.at[j], device_id=place(j), device_id_type=MESH,
            ).wait_recv()
        return carry

    def far_back(j):
        return pltpu.make_async_remote_copy(
            src_ref=bret_s.at[j], dst_ref=bret_r.at[far_head], send_sem=sbr_sem.at[j],
            recv_sem=rbr_sem.at[far_head], device_id=place(j), device_id_type=MESH,
        )

    def far_back_start(j, carry):
        @pl.when(j != mine)
        def _():
            far_back(j).start()
        return carry

    @pl.when(is_far)
    def _():
        recv_b[mine] = send_b[far_head]
        lax.fori_loop(0, n_dev, far_wait, 0)
        q, k, v, g = (recv_b[:, a].reshape(n_dev * nb, LANES) for a in range(4))
        for index, grad in enumerate(head_back(q, k, v, g, k, q, g)):
            bret_s[:, index] = grad.reshape(n_dev, nb, LANES)
        lax.fori_loop(0, n_dev, far_back_start, 0)
        bret_r[far_head] = bret_s[mine]

    done, ready, sent = set(), 0, 0
    for i in range(heads):
        while ready * LANES < (i + 1) * HD:
            for step in range(1, n_in):
                near_copy(ready, step).wait_recv()
            ready += 1
        near_head(i, done)
        while sent < tiles and (sent + 1) * LANES <= (i + 1) * HD:
            for step in range(1, n_in):
                back_copy(sent, step).start()
            ret_r[sent, me] = ret_s[sent, :, me]
            sent += 1

    def far_back_wait(h, carry):
        @pl.when(h * spacing != mine)
        def _():
            pltpu.make_async_remote_copy(
                src_ref=bret_s.at[0], dst_ref=bret_r.at[h], send_sem=sbr_sem.at[0],
                recv_sem=rbr_sem.at[h], device_id=place(h * spacing), device_id_type=MESH,
            ).wait_recv()
            far_copy(h).wait_send()
        return carry

    lax.fori_loop(0, H, far_back_wait, 0)

    far_grads = []
    for index in range(3):
        parts = [bret_r[h, index][:, :HD] for h in range(H)]
        far_grads.append(jnp.concatenate(parts, axis=1))

    for t in range(tiles):
        for step in range(1, n_in):
            back_copy(t, step).wait_recv()
        for p in range(n_in):
            c = p * width + t * LANES
            mask = (row_a == offs[0:1, c:c + LANES]).astype(jnp.float32)
            far_mask = (row_of % stride_b == offs[1:2, c:c + LANES]).astype(jnp.float32)
            for index in range(3):
                near = dot(pick_a, ret_r[t, p, index], ((0,), (0,))) * mask
                far = dot(pick_b, far_grads[index][:, c:c + LANES], ((0,), (0,))) * far_mask
                outs[index][:, c:c + LANES] = (near + far).astype(jnp.bfloat16)

    for t in range(tiles):
        for step in range(1, n_in):
            near_copy(t, step).wait_send()
            back_copy(t, step).wait_send()

    def far_back_sent(j, carry):
        @pl.when(j != mine)
        def _():
            far_back(j).wait_send()
        return carry

    @pl.when(is_far)
    def _():
        lax.fori_loop(0, n_dev, far_back_sent, 0)


def fused(arrays, short_offsets, global_offsets, n_out, n_in, stride_a, stride_b):
    rows = arrays[0].shape[0]
    n_dev = n_out * n_in
    na, nb = rows // stride_a, rows // stride_b
    tiles = D // n_in // LANES
    offs = jnp.repeat(jnp.stack([short_offsets, global_offsets]), HD, axis=1)
    bf16 = jnp.bfloat16
    sem = pltpu.SemaphoreType.DMA
    vmem = pl.BlockSpec(memory_space=pltpu.VMEM)
    return pl.pallas_call(
        functools.partial(kernel, n_out, n_in, stride_a, stride_b),
        out_shape=[jax.ShapeDtypeStruct((rows, D), bf16)] * 3,
        in_specs=[vmem] * 5,
        out_specs=[vmem] * 3,
        scratch_shapes=[
            pltpu.VMEM((tiles, n_in, 4, na, LANES), bf16),
            pltpu.VMEM((tiles, 4, n_in, na, LANES), bf16),
            pltpu.VMEM((tiles, 3, n_in, na, LANES), bf16),
            pltpu.VMEM((tiles, n_in, 3, na, LANES), bf16),
            pltpu.VMEM((H, 4, nb, LANES), bf16),
            pltpu.VMEM((n_dev, 4, nb, LANES), bf16),
            pltpu.VMEM((n_dev, 3, nb, LANES), bf16),
            pltpu.VMEM((H, 3, nb, LANES), bf16),
            sem((tiles, n_in - 1)), sem((tiles, n_in - 1)),
            sem((tiles, n_in - 1)), sem((tiles, n_in - 1)),
            sem((H,)), sem((n_dev,)), sem((n_dev,)), sem((H,)),
        ],
        compiler_params=pltpu.CompilerParams(
            collective_id=0, has_side_effects=True, vmem_limit_bytes=56 * 1024 * 1024
        ),
    )(*arrays, offs)


def solution(mesh):
    n_out, n_in = mesh.shape["outer"], mesh.shape["inner"]

    def local(queries, key_rows, value_rows, upstream, short_offsets, global_offsets):
        arrays = (queries, key_rows, value_rows, upstream)
        rows = queries.shape[0]
        n_dev = n_out * n_in
        stride_a = rows * n_in // KEEP_A
        stride_b = rows * n_dev // KEEP_B
        fits = (rows // stride_b) % 16 == 0 and n_dev % H == 0 and D % (n_in * LANES) == 0
        if fits:
            return tuple(
                fused(arrays, short_offsets, global_offsets, n_out, n_in, stride_a, stride_b)
            )
        return general(arrays, short_offsets, global_offsets, stride_a, stride_b, n_dev)

    rows_spec = P(("outer", "inner"), None)
    return jax.shard_map(
        local, mesh=mesh, in_specs=(rows_spec,) * 4 + (P(), P()), out_specs=(rows_spec,) * 3,
        check_vma=False,
    )
```

```python
import functools
import math

import jax
import jax.numpy as jnp
from jax import lax
from jax.experimental import pallas as pl
from jax.experimental.pallas import tpu as pltpu
from jax.sharding import PartitionSpec as P

H = 16
HD = 96
D = 1536
KEEP_A = 512
KEEP_B = 512
LANES = 128
MESH = pl.DeviceIdType.MESH


def pick_rows(block, offsets, stride):
    count = block.shape[0] // stride
    shaped = block.reshape(count, stride, H, HD)
    onehot = (jnp.arange(stride, dtype=jnp.int32)[:, None] == offsets[None, :]).astype(block.dtype)
    return jnp.sum(shaped * onehot[None, :, :, None], axis=1)


def put_rows(grads, offsets, stride):
    onehot = (jnp.arange(stride, dtype=jnp.int32)[:, None] == offsets[None, :]).astype(jnp.float32)
    spread = grads[:, None, :, :] * onehot[None, :, :, None]
    return spread.reshape(grads.shape[0] * stride, H * HD)


def attend_back(query_part, key_part, value_part, grad_part):
    softmax_scale = HD ** (-0.5)
    scores = (
        jnp.einsum("qhd,khd->hqk", query_part, key_part, preferred_element_type=jnp.float32)
        * softmax_scale
    )
    row_max = jnp.max(scores, axis=-1, keepdims=True)
    weights = jnp.exp(scores - row_max)
    probs = weights / jnp.sum(weights, axis=-1, keepdims=True)
    probs_low = probs.astype(jnp.bfloat16)
    output = jnp.einsum("hqk,khd->qhd", probs_low, value_part, preferred_element_type=jnp.float32)
    delta = jnp.sum(grad_part.astype(jnp.float32) * output, axis=-1)
    dprobs = jnp.einsum("qhd,khd->hqk", grad_part, value_part, preferred_element_type=jnp.float32)
    dscores = (probs * (dprobs - jnp.transpose(delta)[:, :, None])).astype(jnp.bfloat16)
    grad_q = (
        jnp.einsum("hqk,khd->qhd", dscores, key_part, preferred_element_type=jnp.float32)
        * softmax_scale
    )
    grad_k = (
        jnp.einsum("hqk,qhd->khd", dscores, query_part, preferred_element_type=jnp.float32)
        * softmax_scale
    )
    grad_v = jnp.einsum("hqk,qhd->khd", probs_low, grad_part, preferred_element_type=jnp.float32)
    return (grad_q, grad_k, grad_v)


def general(arrays, short_offsets, global_offsets, short_stride, far_stride, n_dev):
    far_count = arrays[0].shape[0] // far_stride
    near = [pick_rows(member, short_offsets, short_stride) for member in arrays]
    split = [lax.all_to_all(m, "inner", split_axis=1, concat_axis=0, tiled=True) for m in near]
    near_grads = attend_back(*split)
    near_final = [
        lax.all_to_all(m, "inner", split_axis=0, concat_axis=1, tiled=True) for m in near_grads
    ]
    far = [pick_rows(m, global_offsets, far_stride).reshape(far_count, D) for m in arrays]
    gathered = [
        lax.all_gather(m, ("outer", "inner"), axis=0, tiled=True).reshape(KEEP_B, 4, H // 4, HD)
        for m in far
    ]
    packed = tuple(jnp.moveaxis(m, 1, 0) for m in gathered)
    mapped = lax.map(lambda pack: attend_back(*pack), packed)
    whole = [jnp.moveaxis(m, 0, 1).reshape(KEEP_B, H, HD) for m in mapped]
    start = lax.axis_index(("outer", "inner")) * far_count
    results = []
    for index in range(3):
        mine = lax.dynamic_slice_in_dim(whole[index], start, far_count, 0)
        total = put_rows(near_final[index], short_offsets, short_stride) + put_rows(
            mine, global_offsets, far_stride
        )
        results.append(total.astype(jnp.bfloat16))
    return tuple(results)


def dot(a, b, dims):
    return lax.dot_general(a, b, (dims, ((), ())), preferred_element_type=jnp.float32)


def head_back(q, k, v, g, km, qm, gm):
    scale = HD ** (-0.5)
    s = dot(km, q, ((1,), (1,)))
    m = jnp.max(s, axis=0, keepdims=True)
    w = jnp.exp2((s - m) * (scale * math.log2(math.e)))
    p = w * (1.0 / jnp.sum(w, axis=0, keepdims=True))
    pb = p.astype(jnp.bfloat16)
    dp = dot(v, gm, ((1,), (1,)))
    delta = jnp.sum(pb.astype(jnp.float32) * dp, axis=0, keepdims=True)
    ds = (p * (dp - delta)).astype(jnp.bfloat16)
    dq = dot(ds, km, ((0,), (0,))) * scale
    dk = dot(ds, qm, ((1,), (0,))) * scale
    dv = dot(pb, gm, ((1,), (0,)))
    return dq.astype(jnp.bfloat16), dk.astype(jnp.bfloat16), dv.astype(jnp.bfloat16)


def picker(count, rows, stride):
    i = lax.broadcasted_iota(jnp.int32, (count, rows), 0)
    r = lax.broadcasted_iota(jnp.int32, (count, rows), 1)
    return (r // stride == i).astype(jnp.bfloat16)


def putter(rows, count, stride):
    r = lax.broadcasted_iota(jnp.int32, (rows, count), 0)
    i = lax.broadcasted_iota(jnp.int32, (rows, count), 1)
    return (r // stride == i).astype(jnp.bfloat16)


def lane_offsets(offsets):
    head = lax.broadcasted_iota(jnp.int32, (1, D), 1) // HD
    spread = jnp.zeros((1, D), jnp.int32)
    for h in range(H):
        spread = jnp.where(head == h, offsets[h], spread)
    return spread


def kernel(
    n_out, n_in, stride_a, stride_b,
    x0, x1, x2, x3, near_offs, far_offs, ret_r, bret_r,
    xs, send_a, recv_a, ret_s, send_b, recv_b, bret_s,
    in_sem, own_sem, sa_sem, ra_sem, sr_sem, rr_sem, sb_sem, rb_sem, sbr_sem, rbr_sem,
):
    loads = [
        pltpu.make_async_copy(x, xs.at[a], in_sem.at[a]) for a, x in enumerate((x0, x1, x2, x3))
    ]
    for load in loads:
        load.start()
    n_dev = n_out * n_in
    spacing = n_dev // H
    mo, me = lax.axis_index("outer"), lax.axis_index("inner")
    mine = mo * n_in + me
    rows = x0.shape[0]
    na, nb = rows // stride_a, rows // stride_b
    width = D // n_in
    tiles = width // LANES
    heads = H // n_in
    far_head = mine // spacing
    is_far = mine % spacing == 0

    def place(index):
        return (index // n_in, index % n_in)

    barrier = pltpu.get_barrier_semaphore()

    def greet(step, carry):
        pl.semaphore_signal(
            barrier, inc=1, device_id=place((mine + step) % n_dev), device_id_type=MESH
        )
        return carry

    lax.fori_loop(1, n_dev, greet, 0)

    row_of = lax.broadcasted_iota(jnp.int32, (rows, LANES), 0)
    pick_a, pick_b = picker(na, rows, stride_a), picker(nb, rows, stride_b)

    def near_copy(t, step):
        peer = (me + step) % n_in
        return pltpu.make_async_remote_copy(
            src_ref=send_a.at[t, peer], dst_ref=recv_a.at[t, :, me],
            send_sem=sa_sem.at[t, step - 1], recv_sem=ra_sem.at[t, step - 1],
            device_id=(mo, peer), device_id_type=MESH,
        )

    def far_copy(h):
        return pltpu.make_async_remote_copy(
            src_ref=send_b.at[h], dst_ref=recv_b.at[mine], send_sem=sb_sem.at[h],
            recv_sem=rb_sem.at[mine], device_id=place(h * spacing), device_id_type=MESH,
        )

    def far_start(h, carry):
        @pl.when(h * spacing != mine)
        def _():
            far_copy(h).start()
        return carry

    off_a, off_b = lane_offsets(near_offs), lane_offsets(far_offs)
    row_a = row_of % stride_a

    def pick_tile(t):
        for p in range(n_in):
            c = p * width + t * LANES
            mask = (row_a == off_a[:, c:c + LANES]).astype(jnp.float32).astype(jnp.bfloat16)
            for a in range(4):
                send_a[t, p, a] = dot(
                    pick_a, xs[a, :, c:c + LANES] * mask, ((1,), (0,))
                ).astype(jnp.bfloat16)
        for a in range(4):
            recv_a[t, a, me] = send_a[t, me, a]

    def start_tile(t):
        for step in range(1, n_in):
            near_copy(t, step).start()

    for load in loads:
        load.wait()
    pick_tile(0)
    pl.semaphore_wait(barrier, n_dev - 1)
    start_tile(0)

    rows_b = lax.broadcasted_iota(jnp.int32, (rows, D), 0) % stride_b
    mask_b = (rows_b == off_b).astype(jnp.float32).astype(jnp.bfloat16)
    for a in range(4):
        far = dot(pick_b, xs[a] * mask_b, ((1,), (0,))).astype(jnp.bfloat16)
        for h in range(H):
            piece = far[:, h * HD:(h + 1) * HD]
            send_b[h, a] = jnp.concatenate(
                [piece, jnp.zeros((nb, LANES - HD), jnp.bfloat16)], axis=1
            )

    lax.fori_loop(0, H, far_start, 0)

    for t in range(1, tiles):
        pick_tile(t)
        start_tile(t)

    def back_copy(t, step):
        peer = (me + step) % n_in
        return pltpu.make_async_remote_copy(
            src_ref=ret_s.at[t, :, peer], dst_ref=ret_r.at[t, me],
            send_sem=sr_sem.at[t, step - 1], recv_sem=rr_sem.at[t, step - 1],
            device_id=(mo, peer), device_id_type=MESH,
        )

    def near_head(i, first):
        lo, hi = i * HD, (i + 1) * HD
        t0, t1 = lo // LANES, (hi - 1) // LANES
        wide = (t1 - t0 + 1) * LANES
        lane = lax.broadcasted_iota(jnp.int32, (1, wide), 1)
        mask = ((lane >= lo - t0 * LANES) & (lane < hi - t0 * LANES)).astype(jnp.float32)
        mask = mask.astype(jnp.bfloat16)

        def whole(a):
            parts = [recv_a[t, a].reshape(n_in * na, LANES) for t in range(t0, t1 + 1)]
            return jnp.concatenate(parts, axis=1) if len(parts) > 1 else parts[0]

        q, k, v, g = (whole(a) for a in range(4))
        grads = head_back(q, k, v, g, k * mask, q * mask, g * mask)
        for index, grad in enumerate(grads):
            for t in range(t0, t1 + 1):
                part = grad[:, (t - t0) * LANES:(t - t0 + 1) * LANES]
                part = part.reshape(n_in, na, LANES)
                if t in first:
                    part = part + ret_s[t, index]
                ret_s[t, index] = part
        first.update(range(t0, t1 + 1))

    def far_wait(j, carry):
        @pl.when(j != mine)
        def _():
            pltpu.make_async_remote_copy(
                src_ref=send_b.at[0], dst_ref=recv_b.at[j], send_sem=sb_sem.at[0],
                recv_sem=rb_sem.at[j], device_id=place(j), device_id_type=MESH,
            ).wait_recv()
        return carry

    def far_back(j):
        return pltpu.make_async_remote_copy(
            src_ref=bret_s.at[j], dst_ref=bret_r.at[far_head], send_sem=sbr_sem.at[j],
            recv_sem=rbr_sem.at[far_head], device_id=place(j), device_id_type=MESH,
        )

    def far_back_start(j, carry):
        @pl.when(j != mine)
        def _():
            far_back(j).start()
        return carry

    def far_own():
        return pltpu.make_async_copy(bret_s.at[mine], bret_r.at[far_head], own_sem.at[tiles])

    def near_own(t):
        return pltpu.make_async_copy(ret_s.at[t, :, me], ret_r.at[t, me], own_sem.at[t])

    def far_whole():
        recv_b[mine] = send_b[far_head]
        lax.fori_loop(0, n_dev, far_wait, 0)
        q, k, v, g = (recv_b[:, a].reshape(n_dev * nb, LANES) for a in range(4))
        for index, grad in enumerate(head_back(q, k, v, g, k, q, g)):
            bret_s[:, index] = grad.reshape(n_dev, nb, LANES)
        lax.fori_loop(0, n_dev, far_back_start, 0)
        far_own().start()

    done, ready, sent = set(), 0, 0
    for i in range(heads):
        while ready * LANES < (i + 1) * HD:
            for step in range(1, n_in):
                near_copy(ready, step).wait_recv()
            ready += 1
        near_head(i, done)
        if i == 0:
            pl.when(is_far)(far_whole)
        while sent < tiles and (sent + 1) * LANES <= (i + 1) * HD:
            for step in range(1, n_in):
                back_copy(sent, step).start()
            near_own(sent).start()
            sent += 1

    def far_back_wait(h, carry):
        @pl.when(h * spacing != mine)
        def _():
            pltpu.make_async_remote_copy(
                src_ref=bret_s.at[0], dst_ref=bret_r.at[h], send_sem=sbr_sem.at[0],
                recv_sem=rbr_sem.at[h], device_id=place(h * spacing), device_id_type=MESH,
            ).wait_recv()
            far_copy(h).wait_send()
        return carry

    lax.fori_loop(0, H, far_back_wait, 0)

    for t in range(tiles):
        near_own(t).wait()
        for step in range(1, n_in):
            back_copy(t, step).wait_recv()

    for t in range(tiles):
        for step in range(1, n_in):
            near_copy(t, step).wait_send()
            back_copy(t, step).wait_send()

    def far_back_sent(j, carry):
        @pl.when(j != mine)
        def _():
            far_back(j).wait_send()
        return carry

    @pl.when(is_far)
    def _():
        lax.fori_loop(0, n_dev, far_back_sent, 0)
        far_own().wait()


def put_kernel(
    stride_a, stride_b, ret_r, bret_r, near_offs, far_offs, o0, o1, o2, made, out_sem
):
    tiles, n_in, _, na, _ = ret_r.shape
    nb = bret_r.shape[2]
    rows = made.shape[1]
    off_a, off_b = lane_offsets(near_offs), lane_offsets(far_offs)
    row_of = lax.broadcasted_iota(jnp.int32, (rows, LANES), 0)
    row_a, row_b = row_of % stride_a, row_of % stride_b
    put_a = putter(rows, na, stride_a)
    put_b = putter(rows, nb, stride_b)
    copies = []
    for index, out in enumerate((o0, o1, o2)):
        parts = [bret_r[h, index][:, :HD] for h in range(H)]
        far_grads = jnp.concatenate(parts, axis=1)
        for t in range(tiles):
            for p in range(n_in):
                c = (p * tiles + t) * LANES
                near = dot(put_a, ret_r[t, p, index], ((1,), (0,)))
                far = dot(put_b, far_grads[:, c:c + LANES], ((1,), (0,)))
                near = jnp.where(row_a == off_a[:, c:c + LANES], near, 0.0)
                far = jnp.where(row_b == off_b[:, c:c + LANES], far, 0.0)
                made[index, :, c:c + LANES] = (near + far).astype(jnp.bfloat16)
        copy = pltpu.make_async_copy(made.at[index], out, out_sem.at[index])
        copy.start()
        copies.append(copy)
    for copy in copies:
        copy.wait()


def fused(arrays, short_offsets, global_offsets, n_out, n_in, stride_a, stride_b):
    rows = arrays[0].shape[0]
    n_dev = n_out * n_in
    na, nb = rows // stride_a, rows // stride_b
    tiles = D // n_in // LANES
    bf16 = jnp.bfloat16
    sem = pltpu.SemaphoreType.DMA
    vmem = pl.BlockSpec(memory_space=pltpu.VMEM)
    smem = pl.BlockSpec(memory_space=pltpu.SMEM)
    whole = pl.BlockSpec(memory_space=pl.ANY)
    limit = 56 * 1024 * 1024
    near, far = pl.pallas_call(
        functools.partial(kernel, n_out, n_in, stride_a, stride_b),
        out_shape=[
            jax.ShapeDtypeStruct((tiles, n_in, 3, na, LANES), bf16),
            jax.ShapeDtypeStruct((H, 3, nb, LANES), bf16),
        ],
        in_specs=[whole] * 4 + [smem] * 2,
        out_specs=[whole] * 2,
        scratch_shapes=[
            pltpu.VMEM((4, rows, D), bf16),
            pltpu.VMEM((tiles, n_in, 4, na, LANES), bf16),
            pltpu.VMEM((tiles, 4, n_in, na, LANES), bf16),
            pltpu.VMEM((tiles, 3, n_in, na, LANES), bf16),
            pltpu.VMEM((H, 4, nb, LANES), bf16),
            pltpu.VMEM((n_dev, 4, nb, LANES), bf16),
            pltpu.VMEM((n_dev, 3, nb, LANES), bf16),
            sem((4,)), sem((tiles + 1,)),
            sem((tiles, n_in - 1)), sem((tiles, n_in - 1)),
            sem((tiles, n_in - 1)), sem((tiles, n_in - 1)),
            sem((H,)), sem((n_dev,)), sem((n_dev,)), sem((H,)),
        ],
        compiler_params=pltpu.CompilerParams(
            collective_id=0, has_side_effects=True, vmem_limit_bytes=limit
        ),
    )(*arrays, short_offsets, global_offsets)
    return pl.pallas_call(
        functools.partial(put_kernel, stride_a, stride_b),
        out_shape=[jax.ShapeDtypeStruct((rows, D), bf16)] * 3,
        in_specs=[vmem] * 2 + [smem] * 2,
        out_specs=[whole] * 3,
        scratch_shapes=[pltpu.VMEM((3, rows, D), bf16), sem((3,))],
        compiler_params=pltpu.CompilerParams(vmem_limit_bytes=limit),
    )(near, far, short_offsets, global_offsets)


def solution(mesh):
    n_out, n_in = mesh.shape["outer"], mesh.shape["inner"]

    def local(queries, key_rows, value_rows, upstream, short_offsets, global_offsets):
        arrays = (queries, key_rows, value_rows, upstream)
        rows = queries.shape[0]
        n_dev = n_out * n_in
        stride_a = rows * n_in // KEEP_A
        stride_b = rows * n_dev // KEEP_B
        fits = (rows // stride_b) % 16 == 0 and n_dev % H == 0 and D % (n_in * LANES) == 0
        if fits:
            return tuple(
                fused(arrays, short_offsets, global_offsets, n_out, n_in, stride_a, stride_b)
            )
        return general(arrays, short_offsets, global_offsets, stride_a, stride_b, n_dev)

    rows_spec = P(("outer", "inner"), None)
    return jax.shard_map(
        local, mesh=mesh, in_specs=(rows_spec,) * 4 + (P(), P()), out_specs=(rows_spec,) * 3,
        check_vma=False,
    )
```

```python
import functools
import math

import jax
import jax.numpy as jnp
from jax import lax
from jax.experimental import pallas as pl
from jax.experimental.pallas import tpu as pltpu
from jax.sharding import PartitionSpec as P

H = 16
HD = 96
D = 1536
KEEP_A = 512
KEEP_B = 512
LANES = 128
MESH = pl.DeviceIdType.MESH


def pick_rows(block, offsets, stride):
    count = block.shape[0] // stride
    shaped = block.reshape(count, stride, H, HD)
    onehot = (jnp.arange(stride, dtype=jnp.int32)[:, None] == offsets[None, :]).astype(block.dtype)
    return jnp.sum(shaped * onehot[None, :, :, None], axis=1)


def put_rows(grads, offsets, stride):
    onehot = (jnp.arange(stride, dtype=jnp.int32)[:, None] == offsets[None, :]).astype(jnp.float32)
    spread = grads[:, None, :, :] * onehot[None, :, :, None]
    return spread.reshape(grads.shape[0] * stride, H * HD)


def attend_back(query_part, key_part, value_part, grad_part):
    softmax_scale = HD ** (-0.5)
    scores = (
        jnp.einsum("qhd,khd->hqk", query_part, key_part, preferred_element_type=jnp.float32)
        * softmax_scale
    )
    row_max = jnp.max(scores, axis=-1, keepdims=True)
    weights = jnp.exp(scores - row_max)
    probs = weights / jnp.sum(weights, axis=-1, keepdims=True)
    probs_low = probs.astype(jnp.bfloat16)
    output = jnp.einsum("hqk,khd->qhd", probs_low, value_part, preferred_element_type=jnp.float32)
    delta = jnp.sum(grad_part.astype(jnp.float32) * output, axis=-1)
    dprobs = jnp.einsum("qhd,khd->hqk", grad_part, value_part, preferred_element_type=jnp.float32)
    dscores = (probs * (dprobs - jnp.transpose(delta)[:, :, None])).astype(jnp.bfloat16)
    grad_q = (
        jnp.einsum("hqk,khd->qhd", dscores, key_part, preferred_element_type=jnp.float32)
        * softmax_scale
    )
    grad_k = (
        jnp.einsum("hqk,qhd->khd", dscores, query_part, preferred_element_type=jnp.float32)
        * softmax_scale
    )
    grad_v = jnp.einsum("hqk,qhd->khd", probs_low, grad_part, preferred_element_type=jnp.float32)
    return (grad_q, grad_k, grad_v)


def general(arrays, short_offsets, global_offsets, short_stride, far_stride, n_dev):
    far_count = arrays[0].shape[0] // far_stride
    near = [pick_rows(member, short_offsets, short_stride) for member in arrays]
    split = [lax.all_to_all(m, "inner", split_axis=1, concat_axis=0, tiled=True) for m in near]
    near_grads = attend_back(*split)
    near_final = [
        lax.all_to_all(m, "inner", split_axis=0, concat_axis=1, tiled=True) for m in near_grads
    ]
    far = [pick_rows(m, global_offsets, far_stride).reshape(far_count, D) for m in arrays]
    gathered = [
        lax.all_gather(m, ("outer", "inner"), axis=0, tiled=True).reshape(KEEP_B, 4, H // 4, HD)
        for m in far
    ]
    packed = tuple(jnp.moveaxis(m, 1, 0) for m in gathered)
    mapped = lax.map(lambda pack: attend_back(*pack), packed)
    whole = [jnp.moveaxis(m, 0, 1).reshape(KEEP_B, H, HD) for m in mapped]
    start = lax.axis_index(("outer", "inner")) * far_count
    results = []
    for index in range(3):
        mine = lax.dynamic_slice_in_dim(whole[index], start, far_count, 0)
        total = put_rows(near_final[index], short_offsets, short_stride) + put_rows(
            mine, global_offsets, far_stride
        )
        results.append(total.astype(jnp.bfloat16))
    return tuple(results)


def dot(a, b, dims):
    return lax.dot_general(a, b, (dims, ((), ())), preferred_element_type=jnp.float32)


def head_back(q, k, v, g, km, qm, gm):
    scale = HD ** (-0.5)
    s = dot(km, q, ((1,), (1,)))
    m = jnp.max(s, axis=0, keepdims=True)
    w = jnp.exp2((s - m) * (scale * math.log2(math.e)))
    p = w * (1.0 / jnp.sum(w, axis=0, keepdims=True))
    pb = p.astype(jnp.bfloat16)
    dp = dot(v, gm, ((1,), (1,)))
    delta = jnp.sum(pb.astype(jnp.float32) * dp, axis=0, keepdims=True)
    ds = (p * (dp - delta)).astype(jnp.bfloat16)
    dq = dot(ds, km, ((0,), (0,))) * scale
    dk = dot(ds, qm, ((1,), (0,))) * scale
    dv = dot(pb, gm, ((1,), (0,)))
    return dq.astype(jnp.bfloat16), dk.astype(jnp.bfloat16), dv.astype(jnp.bfloat16)


def picker(count, rows, stride):
    i = lax.broadcasted_iota(jnp.int32, (count, rows), 0)
    r = lax.broadcasted_iota(jnp.int32, (count, rows), 1)
    return (r // stride == i).astype(jnp.bfloat16)


def putter(rows, count, stride):
    r = lax.broadcasted_iota(jnp.int32, (rows, count), 0)
    i = lax.broadcasted_iota(jnp.int32, (rows, count), 1)
    return (r // stride == i).astype(jnp.bfloat16)


def lane_offsets(offsets):
    head = lax.broadcasted_iota(jnp.int32, (1, D), 1) // HD
    spread = jnp.zeros((1, D), jnp.int32)
    for h in range(H):
        spread = jnp.where(head == h, offsets[h], spread)
    return spread


def kernel(
    n_out, n_in, stride_a, stride_b,
    x0, x1, x2, x3, near_offs, far_offs, ret_r, bret_r,
    xs, send_a, recv_a, ret_s, send_b, recv_b, bret_s,
    in_sem, own_sem, sa_sem, ra_sem, sr_sem, rr_sem, sb_sem, rb_sem, sbr_sem, rbr_sem,
):
    loads = [
        pltpu.make_async_copy(x, xs.at[a], in_sem.at[a]) for a, x in enumerate((x0, x1, x2, x3))
    ]
    for load in loads:
        load.start()
    n_dev = n_out * n_in
    spacing = n_dev // H
    mo, me = lax.axis_index("outer"), lax.axis_index("inner")
    mine = mo * n_in + me
    rows = x0.shape[0]
    na, nb = rows // stride_a, rows // stride_b
    width = D // n_in
    tiles = width // LANES
    heads = H // n_in
    far_head = mine // spacing
    is_far = mine % spacing == 0

    def place(index):
        return (index // n_in, index % n_in)

    barrier = pltpu.get_barrier_semaphore()

    def greet(step, carry):
        pl.semaphore_signal(
            barrier, inc=1, device_id=place((mine + step) % n_dev), device_id_type=MESH
        )
        return carry

    lax.fori_loop(1, n_dev, greet, 0)

    row_of = lax.broadcasted_iota(jnp.int32, (rows, LANES), 0)
    pick_a, pick_b = picker(na, rows, stride_a), picker(nb, rows, stride_b)

    def near_copy(t, step):
        peer = (me + step) % n_in
        return pltpu.make_async_remote_copy(
            src_ref=send_a.at[t, peer], dst_ref=recv_a.at[t, :, me],
            send_sem=sa_sem.at[t, step - 1], recv_sem=ra_sem.at[t, step - 1],
            device_id=(mo, peer), device_id_type=MESH,
        )

    def far_copy(h):
        return pltpu.make_async_remote_copy(
            src_ref=send_b.at[h], dst_ref=recv_b.at[mine], send_sem=sb_sem.at[h],
            recv_sem=rb_sem.at[mine], device_id=place(h * spacing), device_id_type=MESH,
        )

    def far_start(h, carry):
        @pl.when(h * spacing != mine)
        def _():
            far_copy(h).start()
        return carry

    off_a, off_b = lane_offsets(near_offs), lane_offsets(far_offs)
    row_a = row_of % stride_a

    def pick_tile(t):
        for p in range(n_in):
            c = p * width + t * LANES
            mask = (row_a == off_a[:, c:c + LANES]).astype(jnp.float32).astype(jnp.bfloat16)
            for a in range(4):
                send_a[t, p, a] = dot(
                    pick_a, xs[a, :, c:c + LANES] * mask, ((1,), (0,))
                ).astype(jnp.bfloat16)
        for a in range(4):
            recv_a[t, a, me] = send_a[t, me, a]

    def start_tile(t):
        for step in range(1, n_in):
            near_copy(t, step).start()

    for load in loads:
        load.wait()
    pick_tile(0)
    pl.semaphore_wait(barrier, n_dev - 1)
    start_tile(0)

    rows_b = lax.broadcasted_iota(jnp.int32, (rows, D), 0) % stride_b
    mask_b = (rows_b == off_b).astype(jnp.float32).astype(jnp.bfloat16)
    fars = []
    for a in range(4):
        far = dot(pick_b, xs[a] * mask_b, ((1,), (0,))).astype(jnp.bfloat16)
        fars.append(far)
    for h in range(H):
        packed = jnp.concatenate([far[:, h * HD:(h + 1) * HD] for far in fars], axis=1)
        for t in range(4 * HD // LANES):
            send_b[h, t] = packed[:, t * LANES:(t + 1) * LANES]

    lax.fori_loop(0, H, far_start, 0)

    for t in range(1, tiles):
        pick_tile(t)
        start_tile(t)

    def back_copy(t, step):
        peer = (me + step) % n_in
        return pltpu.make_async_remote_copy(
            src_ref=ret_s.at[t, :, peer], dst_ref=ret_r.at[t, me],
            send_sem=sr_sem.at[t, step - 1], recv_sem=rr_sem.at[t, step - 1],
            device_id=(mo, peer), device_id_type=MESH,
        )

    def near_head(i, first):
        lo, hi = i * HD, (i + 1) * HD
        t0, t1 = lo // LANES, (hi - 1) // LANES
        wide = (t1 - t0 + 1) * LANES
        lane = lax.broadcasted_iota(jnp.int32, (1, wide), 1)
        mask = ((lane >= lo - t0 * LANES) & (lane < hi - t0 * LANES)).astype(jnp.float32)
        mask = mask.astype(jnp.bfloat16)

        def whole(a):
            parts = [recv_a[t, a].reshape(n_in * na, LANES) for t in range(t0, t1 + 1)]
            return jnp.concatenate(parts, axis=1) if len(parts) > 1 else parts[0]

        q, k, v, g = (whole(a) for a in range(4))
        grads = head_back(q, k, v, g, k * mask, q * mask, g * mask)
        for index, grad in enumerate(grads):
            for t in range(t0, t1 + 1):
                part = grad[:, (t - t0) * LANES:(t - t0 + 1) * LANES]
                part = part.reshape(n_in, na, LANES)
                if t in first:
                    part = part + ret_s[t, index]
                ret_s[t, index] = part
        first.update(range(t0, t1 + 1))

    def far_wait(j, carry):
        @pl.when(j != mine)
        def _():
            pltpu.make_async_remote_copy(
                src_ref=send_b.at[0], dst_ref=recv_b.at[j], send_sem=sb_sem.at[0],
                recv_sem=rb_sem.at[j], device_id=place(j), device_id_type=MESH,
            ).wait_recv()
        return carry

    def far_back(j):
        return pltpu.make_async_remote_copy(
            src_ref=bret_s.at[j], dst_ref=bret_r.at[far_head], send_sem=sbr_sem.at[j],
            recv_sem=rbr_sem.at[far_head], device_id=place(j), device_id_type=MESH,
        )

    def far_back_start(j, carry):
        @pl.when(j != mine)
        def _():
            far_back(j).start()
        return carry

    def far_own():
        return pltpu.make_async_copy(bret_s.at[mine], bret_r.at[far_head], own_sem.at[tiles])

    def near_own(t):
        return pltpu.make_async_copy(ret_s.at[t, :, me], ret_r.at[t, me], own_sem.at[t])

    def far_whole():
        recv_b[mine] = send_b[far_head]
        lax.fori_loop(0, n_dev, far_wait, 0)
        packed = jnp.concatenate(
            [recv_b[:, t].reshape(n_dev * nb, LANES) for t in range(4 * HD // LANES)], axis=1
        )
        q, k, v, g = (packed[:, a * HD:(a + 1) * HD] for a in range(4))
        pad = jnp.zeros((n_dev * nb, LANES - HD), jnp.bfloat16)
        for index, grad in enumerate(head_back(q, k, v, g, k, q, g)):
            bret_s[:, index] = jnp.concatenate([grad, pad], axis=1).reshape(n_dev, nb, LANES)
        lax.fori_loop(0, n_dev, far_back_start, 0)
        far_own().start()

    done, ready, sent = set(), 0, 0
    for i in range(heads):
        while ready * LANES < (i + 1) * HD:
            for step in range(1, n_in):
                near_copy(ready, step).wait_recv()
            ready += 1
        near_head(i, done)
        if i == 0:
            pl.when(is_far)(far_whole)
        while sent < tiles and (sent + 1) * LANES <= (i + 1) * HD:
            for step in range(1, n_in):
                back_copy(sent, step).start()
            near_own(sent).start()
            sent += 1

    def far_back_wait(h, carry):
        @pl.when(h * spacing != mine)
        def _():
            pltpu.make_async_remote_copy(
                src_ref=bret_s.at[0], dst_ref=bret_r.at[h], send_sem=sbr_sem.at[0],
                recv_sem=rbr_sem.at[h], device_id=place(h * spacing), device_id_type=MESH,
            ).wait_recv()
            far_copy(h).wait_send()
        return carry

    lax.fori_loop(0, H, far_back_wait, 0)

    for t in range(tiles):
        near_own(t).wait()
        for step in range(1, n_in):
            back_copy(t, step).wait_recv()

    for t in range(tiles):
        for step in range(1, n_in):
            near_copy(t, step).wait_send()
            back_copy(t, step).wait_send()

    def far_back_sent(j, carry):
        @pl.when(j != mine)
        def _():
            far_back(j).wait_send()
        return carry

    @pl.when(is_far)
    def _():
        lax.fori_loop(0, n_dev, far_back_sent, 0)
        far_own().wait()


def put_kernel(
    stride_a, stride_b, near_ref, bret_r, near_offs, far_offs, o0, o1, o2, ret_r, made, in_sem, out_sem
):
    tiles, n_in, _, na, _ = near_ref.shape
    loads = [
        pltpu.make_async_copy(near_ref.at[:, :, index], ret_r.at[index], in_sem.at[index])
        for index in range(3)
    ]
    for load in loads:
        load.start()
    nb = bret_r.shape[2]
    rows = made.shape[1]
    off_a, off_b = lane_offsets(near_offs), lane_offsets(far_offs)
    row_of = lax.broadcasted_iota(jnp.int32, (rows, LANES), 0)
    row_a, row_b = row_of % stride_a, row_of % stride_b
    put_a = putter(rows, na, stride_a)
    put_b = putter(rows, nb, stride_b)
    copies = []
    for index, out in enumerate((o0, o1, o2)):
        parts = [bret_r[h, index][:, :HD] for h in range(H)]
        far_grads = jnp.concatenate(parts, axis=1)
        loads[index].wait()
        for t in range(tiles):
            for p in range(n_in):
                c = (p * tiles + t) * LANES
                near = dot(put_a, ret_r[index, t, p], ((1,), (0,)))
                far = dot(put_b, far_grads[:, c:c + LANES], ((1,), (0,)))
                near = jnp.where(row_a == off_a[:, c:c + LANES], near, 0.0)
                far = jnp.where(row_b == off_b[:, c:c + LANES], far, 0.0)
                made[index, :, c:c + LANES] = (near + far).astype(jnp.bfloat16)
        copy = pltpu.make_async_copy(made.at[index], out, out_sem.at[index])
        copy.start()
        copies.append(copy)
    for copy in copies:
        copy.wait()


def fused(arrays, short_offsets, global_offsets, n_out, n_in, stride_a, stride_b):
    rows = arrays[0].shape[0]
    n_dev = n_out * n_in
    na, nb = rows // stride_a, rows // stride_b
    tiles = D // n_in // LANES
    bf16 = jnp.bfloat16
    sem = pltpu.SemaphoreType.DMA
    vmem = pl.BlockSpec(memory_space=pltpu.VMEM)
    smem = pl.BlockSpec(memory_space=pltpu.SMEM)
    whole = pl.BlockSpec(memory_space=pl.ANY)
    limit = 56 * 1024 * 1024
    near, far = pl.pallas_call(
        functools.partial(kernel, n_out, n_in, stride_a, stride_b),
        out_shape=[
            jax.ShapeDtypeStruct((tiles, n_in, 3, na, LANES), bf16),
            jax.ShapeDtypeStruct((H, 3, nb, LANES), bf16),
        ],
        in_specs=[whole] * 4 + [smem] * 2,
        out_specs=[whole] * 2,
        scratch_shapes=[
            pltpu.VMEM((4, rows, D), bf16),
            pltpu.VMEM((tiles, n_in, 4, na, LANES), bf16),
            pltpu.VMEM((tiles, 4, n_in, na, LANES), bf16),
            pltpu.VMEM((tiles, 3, n_in, na, LANES), bf16),
            pltpu.VMEM((H, 4 * HD // LANES, nb, LANES), bf16),
            pltpu.VMEM((n_dev, 4 * HD // LANES, nb, LANES), bf16),
            pltpu.VMEM((n_dev, 3, nb, LANES), bf16),
            sem((4,)), sem((tiles + 1,)),
            sem((tiles, n_in - 1)), sem((tiles, n_in - 1)),
            sem((tiles, n_in - 1)), sem((tiles, n_in - 1)),
            sem((H,)), sem((n_dev,)), sem((n_dev,)), sem((H,)),
        ],
        compiler_params=pltpu.CompilerParams(
            collective_id=0, has_side_effects=True, vmem_limit_bytes=limit
        ),
    )(*arrays, short_offsets, global_offsets)
    return pl.pallas_call(
        functools.partial(put_kernel, stride_a, stride_b),
        out_shape=[jax.ShapeDtypeStruct((rows, D), bf16)] * 3,
        in_specs=[whole, vmem] + [smem] * 2,
        out_specs=[whole] * 3,
        scratch_shapes=[
            pltpu.VMEM((3, tiles, n_in, na, LANES), bf16),
            pltpu.VMEM((3, rows, D), bf16), sem((3,)), sem((3,)),
        ],
        compiler_params=pltpu.CompilerParams(vmem_limit_bytes=limit),
    )(near, far, short_offsets, global_offsets)


def solution(mesh):
    n_out, n_in = mesh.shape["outer"], mesh.shape["inner"]

    def local(queries, key_rows, value_rows, upstream, short_offsets, global_offsets):
        arrays = (queries, key_rows, value_rows, upstream)
        rows = queries.shape[0]
        n_dev = n_out * n_in
        stride_a = rows * n_in // KEEP_A
        stride_b = rows * n_dev // KEEP_B
        fits = (rows // stride_b) % 16 == 0 and n_dev % H == 0 and D % (n_in * LANES) == 0
        if fits:
            return tuple(
                fused(arrays, short_offsets, global_offsets, n_out, n_in, stride_a, stride_b)
            )
        return general(arrays, short_offsets, global_offsets, stride_a, stride_b, n_dev)

    rows_spec = P(("outer", "inner"), None)
    return jax.shard_map(
        local, mesh=mesh, in_specs=(rows_spec,) * 4 + (P(), P()), out_specs=(rows_spec,) * 3,
        check_vma=False,
    )
```
